256 devices in a mesh: lon: 8 (over z_hi, core), lat: 32 (over x, z_lo, y).
Axes of the slice: x: 4, y: 4, z: 8 (z_hi: 4, z_lo: 2; z = z_hi * 2 + z_lo), core: 2. Of those that a mesh axis runs over, the one named last changes fastest.
Arguments:
- observed: float32 [512, 512, 256], P('lon', 'lat'), may hold values from -6 to 6
- prior_draw: float32 [512, 512, 256], P('lon', 'lat'), may hold values from -6 to 6
- noise_draw: float32 [512, 512, 256], P('lon', 'lat'), may hold values from -6 to 6
- basis_lon: float32 [512, 512], replicated, may hold values from -0.25 to 0.25
- basis_lat: float32 [512, 512], replicated, may hold values from -0.25 to 0.25
- basis_time: float32 [256, 256], replicated, may hold values from -0.375 to 0.375
- eig_lon: float32 [512], replicated, may hold values from 0.2 to 5
- eig_lat: float32 [512], replicated, may hold values from 0.2 to 5
- eig_time: float32 [256], replicated, may hold values from 0.2 to 5
Outputs:
- weights: float32 [512, 512, 256], P('lon', 'lat')
- sample: float32 [512, 512, 256], P('lon', 'lat')
The draws below stay inside these ranges and needn't reach their ends.
All inputs are finite; a program needn't handle non-finite values.
Results may differ from the reference program's by a relative error of at most 0.000068.
Values sent between devices are 32-bit elements; how exact they have to be, the bound alone decides.
No kernel may reach another device: no remote copies, remote signals or barrier semaphores. Data moves between devices by JAX's collectives and lax.ppermute only.
A program may use at most 128 MiB of HBM per device.

```python
import math
import jax
import jax.numpy as jnp
from jax import lax

NLON = 512
NLAT = 512
NT = 256


def shard_levels(key, dims, cuts, smallest, largest):
    loudness, own = 1.0, jax.random.fold_in(key, 6)
    for dim, parts in cuts:
        heights = jnp.exp(jax.random.uniform(jax.random.fold_in(own, dim), (parts,), jnp.float32, smallest / len(cuts), largest / len(cuts)))
        loudness = loudness * jnp.repeat(heights, dims[dim] // parts).reshape([-1 if axis == dim else 1 for axis in range(len(dims))])
    return loudness


def normal_values(stream_key, extent, spread, reach, split=(), kind=jnp.bfloat16):
    entries = spread * jax.random.normal(stream_key, extent, jnp.float32)
    if split:
        entries = entries * shard_levels(stream_key, extent, split, -0.22, 0.18)
    return jnp.clip(entries, -reach, reach).astype(kind)


def setup_inputs(seed: int = 0) -> dict:
    splits = jax.random.split(jax.random.key(seed), 10)
    return {
        "observed": normal_values(splits[0], (NLON, NLAT, NT), 1.0, 6.0, ((0, 8), (1, 32)), jnp.float32),
        "prior_draw": normal_values(splits[1], (NLON, NLAT, NT), 1.0, 6.0, ((0, 8), (1, 32)), jnp.float32),
        "noise_draw": normal_values(splits[2], (NLON, NLAT, NT), 1.0, 6.0, ((0, 8), (1, 32)), jnp.float32),
        "basis_lon": normal_values(splits[3], (NLON, NLON), NLON ** -0.5, 0.25, (), jnp.float32),
        "basis_lat": normal_values(splits[4], (NLAT, NLAT), NLAT ** -0.5, 0.25, (), jnp.float32),
        "basis_time": normal_values(splits[5], (NT, NT), NT ** -0.5, 0.375, (), jnp.float32),
        "eig_lon": jnp.clip(jnp.exp(jax.random.uniform(splits[6], (NLON,), jnp.float32, math.log(0.2), math.log(5.0))), 0.2, 5.0),
        "eig_lat": jnp.clip(jnp.exp(jax.random.uniform(splits[7], (NLAT,), jnp.float32, math.log(0.2), math.log(5.0))), 0.2, 5.0),
        "eig_time": jnp.clip(jnp.exp(jax.random.uniform(splits[8], (NT,), jnp.float32, math.log(0.2), math.log(5.0))), 0.2, 5.0),
    }


NOISE_VAR = 0.25
NOISE_STD = 0.5

def forward(field, basis_lon, basis_lat, basis_time):
    hp = lax.Precision.HIGHEST
    field = jnp.einsum('ijk,kc->ijc', field, basis_time, precision=hp, preferred_element_type=jnp.float32)
    field = jnp.einsum('ijc,jb->ibc', field, basis_lat, precision=hp, preferred_element_type=jnp.float32)
    return jnp.einsum('ibc,ia->abc', field, basis_lon, precision=hp, preferred_element_type=jnp.float32)

def backward(field, basis_lon, basis_lat, basis_time):
    hp = lax.Precision.HIGHEST
    field = jnp.einsum('abc,ia->ibc', field, basis_lon, precision=hp, preferred_element_type=jnp.float32)
    field = jnp.einsum('ibc,jb->ijc', field, basis_lat, precision=hp, preferred_element_type=jnp.float32)
    return jnp.einsum('ijc,kc->ijk', field, basis_time, precision=hp, preferred_element_type=jnp.float32)

def reference(observed, prior_draw, noise_draw, basis_lon, basis_lat, basis_time, eig_lon, eig_lat, eig_time):
    spectrum = eig_lon[:, None, None] * eig_lat[None, :, None] * eig_time[None, None, :]
    obs_hat = forward(observed, basis_lon, basis_lat, basis_time)
    shift_hat = forward(observed - NOISE_STD * noise_draw, basis_lon, basis_lat, basis_time)
    denom = spectrum + NOISE_VAR
    weight_hat = obs_hat / denom
    sample_hat = jnp.sqrt(spectrum) * NOISE_VAR / denom * prior_draw + spectrum / denom * shift_hat
    weights = backward(weight_hat, basis_lon, basis_lat, basis_time)
    sample = backward(sample_hat, basis_lon, basis_lat, basis_time)
    return (weights, sample)
```

```python
import functools

import jax
import jax.numpy as jnp
from jax import lax
from jax.experimental import pallas as pl
from jax.experimental.pallas import tpu as pltpu
from jax.sharding import PartitionSpec as P

NOISE_VAR = 0.25
NOISE_STD = 0.5
BF16 = jnp.bfloat16
F32 = jnp.float32
VMEM = pl.BlockSpec(memory_space=pltpu.VMEM)
SMEM = pl.BlockSpec(memory_space=pltpu.SMEM)
NN = (((1,), (0,)), ((), ()))
NT = (((1,), (1,)), ((), ()))
TN = (((0,), (0,)), ((), ()))
PARAMS = pltpu.CompilerParams(vmem_limit_bytes=48 * 1024 * 1024)


def halves(value):
    high = value.astype(BF16)
    low = (value - high.astype(F32)).astype(BF16)
    return high, low


def product(left, right, dims):
    dot = functools.partial(
        lax.dot_general, dimension_numbers=dims, preferred_element_type=F32
    )
    return dot(left[0], right[0]) + (dot(left[0], right[1]) + dot(left[1], right[0]))


def interleave(first, second):
    lanes = lax.broadcasted_iota(jnp.int32, first.shape, 1)
    lower = lanes < 64
    return (
        jnp.where(lower, first, pltpu.roll(second, 64, 1)),
        jnp.where(lower, pltpu.roll(first, 64, 1), second),
    )


def bases_kernel(lon_ref, lat_ref, time_ref, lon_out, lont_out, lat_out, latt_out, time_out):
    for source, plain, flipped in (
        (lon_ref, lon_out, lont_out),
        (lat_ref, lat_out, latt_out),
    ):
        high, low = halves(source[...])
        plain[0], plain[1] = high, low
        high, low = halves(source[...].T)
        flipped[0], flipped[1] = high, low
    time_out[0], time_out[1] = halves(time_ref[...])


def forward_kernel(obs0, obs1, noise0, noise1, prior0, prior1, time_ref, out_ref):
    basis = halves(time_ref[...].T)

    def step(jj, carry):
        rows = pl.ds(jj, 64, stride=16)
        obs = jnp.concatenate([obs0[rows, :], obs1[rows, :]], axis=1)
        noise = jnp.concatenate([noise0[rows, :], noise1[rows, :]], axis=1)
        field = jnp.concatenate([obs, obs - NOISE_STD * noise], axis=0)
        out_ref[pl.ds(jj, 256, stride=24), :] = product(basis, halves(field), NT)
        return carry

    lax.fori_loop(0, 16, step, 0)

    def move(jj, carry):
        for half, prior in enumerate((prior0, prior1)):
            both = jnp.concatenate(
                [prior[pl.ds(jj, 64, stride=16), :], prior[pl.ds(jj + 8, 64, stride=16), :]],
                axis=0,
            )
            out_ref[pl.ds(half * 3072 + 16 + jj, 128, stride=24), :] = both.T
        return carry

    lax.fori_loop(0, 8, move, 0)


def middle_kernel(
    in_ref, lon_ref, lont_ref, lat_ref, latt_ref, vals_lon, vals_lat, val_time, out_ref,
    x_ref, y_ref, prior_ref, scaled_ref, v_ref,
):
    for p in range(4):
        def gather(blk, carry):
            rows = pl.ds(pl.multiple_of(blk * 128, 128), 128)
            even = pl.ds(p * 64 + blk * 8, 8)
            odd = pl.ds(p * 64 + 32 + blk * 8, 8)
            pair = interleave(
                in_ref[even, 0:16, :].reshape(128, 128), in_ref[odd, 0:16, :].reshape(128, 128)
            )
            for f in range(2):
                high, low = halves(pair[f])
                x_ref[0, rows, f * 512 + p * 128:f * 512 + (p + 1) * 128] = high
                x_ref[1, rows, f * 512 + p * 128:f * 512 + (p + 1) * 128] = low
            first, second = interleave(
                in_ref[even, 16:24, :].reshape(64, 128), in_ref[odd, 16:24, :].reshape(64, 128)
            )
            both = jnp.concatenate([first.reshape(8, 8, 128), second.reshape(8, 8, 128)], axis=1)
            prior_ref[rows, p * 128:(p + 1) * 128] = both.reshape(128, 128)
            return carry

        lax.fori_loop(0, 4, gather, 0)

    def lat_forward(n, carry):
        lanes = pl.ds(pl.multiple_of(n * 256, 256), 256)
        result = product(
            (latt_ref[0], latt_ref[1]), (x_ref[0, :, lanes], x_ref[1, :, lanes]), NN
        )
        y_ref[0, :, lanes], y_ref[1, :, lanes] = halves(result)
        return carry

    lax.fori_loop(0, 4, lat_forward, 0)

    def lon_forward(n, carry):
        lanes = pl.ds(pl.multiple_of(n * 256, 256), 256)
        right = (lon_ref[0, :, lanes], lon_ref[1, :, lanes])
        spectrum = vals_lon[:, lanes] * vals_lat[...] * val_time[0]
        denom = spectrum + NOISE_VAR
        hat = product((y_ref[0, :, 0:512], y_ref[1, :, 0:512]), right, NN)
        scaled_ref[0, 0, :, lanes], scaled_ref[0, 1, :, lanes] = halves(hat / denom)
        hat = product((y_ref[0, :, 512:1024], y_ref[1, :, 512:1024]), right, NN)
        sample = (
            jnp.sqrt(spectrum) * NOISE_VAR / denom * prior_ref[:, lanes] + spectrum / denom * hat
        )
        scaled_ref[1, 0, :, lanes], scaled_ref[1, 1, :, lanes] = halves(sample)
        return carry

    lax.fori_loop(0, 2, lon_forward, 0)

    for f in range(2):
        def lon_backward(n, carry):
            lanes = pl.ds(pl.multiple_of(n * 256, 256), 256)
            result = product(
                (scaled_ref[f, 0], scaled_ref[f, 1]), (lont_ref[0, :, lanes], lont_ref[1, :, lanes]), NN
            )
            high, low = halves(result)
            for half in range(2):
                target = pl.ds(pl.multiple_of(n * 512 + half * 256 + f * 128, 128), 128)
                v_ref[0, :, target] = high[:, half * 128:(half + 1) * 128]
                v_ref[1, :, target] = low[:, half * 128:(half + 1) * 128]
            return carry

        lax.fori_loop(0, 2, lon_backward, 0)

    def lat_backward(p, carry):
        lanes = pl.ds(pl.multiple_of(p * 256, 256), 256)
        result = product((lat_ref[0], lat_ref[1]), (v_ref[0, :, lanes], v_ref[1, :, lanes]), NN)
        even, odd = interleave(result[:, :128], result[:, 128:])
        out_ref[pl.ds(p * 64, 32)] = even.reshape(32, 16, 128)
        out_ref[pl.ds(p * 64 + 32, 32)] = odd.reshape(32, 16, 128)
        return carry

    lax.fori_loop(0, 4, lat_backward, 0)


def backward_kernel(in_ref, time_ref, weights_ref, sample_ref):
    basis = (time_ref[0], time_ref[1])

    def step(jj, carry):
        right = halves(in_ref[pl.ds(jj, 256, stride=16), :])
        result = product(basis, right, NN).T
        weights_ref[pl.ds(jj, 64, stride=16), :] = result[:64]
        sample_ref[pl.ds(jj, 64, stride=16), :] = result[64:]
        return carry

    lax.fori_loop(0, 16, step, 0)


def shape(dims, kind=F32):
    return jax.ShapeDtypeStruct(dims, kind)


def cost(flops, nbytes):
    return pl.CostEstimate(flops=int(flops), bytes_accessed=int(nbytes), transcendentals=0)


def on_device(
    observed, prior_draw, noise_draw, basis_lon, basis_lat, basis_time, eig_lon, eig_lat, eig_time
):
    index = lax.axis_index("lon") * 32 + lax.axis_index("lat")
    val_time = lax.dynamic_slice_in_dim(eig_time, index, 1)
    mib = 1 << 20

    lon, lont, lat, latt, time = pl.pallas_call(
        bases_kernel,
        out_shape=[shape((2, 512, 512), BF16)] * 4 + [shape((2, 256, 256), BF16)],
        in_specs=[VMEM] * 3,
        out_specs=[VMEM] * 5,
        compiler_params=PARAMS,
        cost_estimate=cost(4 * mib, 8 * mib),
        name="bases",
    )(basis_lon, basis_lat, basis_time)

    fields = [
        field.reshape(1024, 256)
        for field in (observed, observed, noise_draw, noise_draw, prior_draw, prior_draw)
    ]
    lanes0 = pl.BlockSpec((1024, 128), lambda step: (0, 0))
    lanes1 = pl.BlockSpec((1024, 128), lambda step: (0, 1))
    packed = pl.pallas_call(
        forward_kernel,
        out_shape=shape((6144, 128)),
        grid=(1,),
        in_specs=[lanes0, lanes1] * 3 + [VMEM],
        out_specs=VMEM,
        compiler_params=PARAMS,
        cost_estimate=cost(3 * 2 * 2048 * 256 * 256, 6 * mib),
        name="time_forward",
    )(*fields, basis_time)
    packed = lax.all_to_all(packed.reshape(256, 24, 128), ("lon", "lat"), 0, 0, tiled=True)

    planes = pl.pallas_call(
        middle_kernel,
        out_shape=shape((256, 16, 128)),
        in_specs=[VMEM] * 7 + [SMEM],
        out_specs=VMEM,
        scratch_shapes=[
            pltpu.VMEM((2, 512, 1024), BF16),
            pltpu.VMEM((2, 512, 1024), BF16),
            pltpu.VMEM((512, 512), F32),
            pltpu.VMEM((2, 2, 512, 512), BF16),
            pltpu.VMEM((2, 512, 1024), BF16),
        ],
        compiler_params=PARAMS,
        cost_estimate=cost(3 * 2 * 8 * 512**3, 8 * mib),
        name="middle",
    )(packed, lon, lont, lat, latt, eig_lon.reshape(1, 512), eig_lat.reshape(512, 1), val_time)
    planes = lax.all_to_all(planes, ("lon", "lat"), 0, 0, tiled=True)

    weights, sample = pl.pallas_call(
        backward_kernel,
        out_shape=[shape((1024, 256))] * 2,
        grid=(2,),
        in_specs=[
            pl.BlockSpec((4096, 128), lambda half: (0, 0)),
            pl.BlockSpec((2, 128, 256), lambda half: (0, half, 0)),
        ],
        out_specs=[pl.BlockSpec((1024, 128), lambda half: (0, half))] * 2,
        compiler_params=PARAMS,
        cost_estimate=cost(3 * 2 * 2048 * 256 * 256, 4 * mib),
        name="time_backward",
    )(planes.reshape(4096, 128), time)
    return weights.reshape(64, 16, 256), sample.reshape(64, 16, 256)


def solution(mesh):
    block = P("lon", "lat", None)
    return jax.shard_map(
        on_device,
        mesh=mesh,
        in_specs=(block,) * 3 + (P(),) * 6,
        out_specs=(block, block),
        check_vma=False,
    )
```

```python
import functools

import jax
import jax.numpy as jnp
from jax import lax
from jax.experimental import pallas as pl
from jax.experimental.pallas import tpu as pltpu
from jax.sharding import PartitionSpec as P

NOISE_VAR = 0.25
NOISE_STD = 0.5
BF16 = jnp.bfloat16
F32 = jnp.float32
MIB = 1 << 20
VMEM = pl.BlockSpec(memory_space=pltpu.VMEM)
SMEM = pl.BlockSpec(memory_space=pltpu.SMEM)
ANY = pl.BlockSpec(memory_space=pl.ANY)
NN = (((1,), (0,)), ((), ()))
NT = (((1,), (1,)), ((), ()))


def halves(value):
    high = value.astype(BF16)
    low = (value - high.astype(F32)).astype(BF16)
    return high, low


def product(left, right, dims):
    dot = functools.partial(
        lax.dot_general, dimension_numbers=dims, preferred_element_type=F32
    )
    return dot(left[0], right[0]) + (dot(left[0], right[1]) + dot(left[1], right[0]))


def interleave(first, second):
    lanes = lax.broadcasted_iota(jnp.int32, first.shape, 1)
    lower = lanes < 64
    return (
        jnp.where(lower, first, pltpu.roll(second, 64, 1)),
        jnp.where(lower, pltpu.roll(first, 64, 1), second),
    )


def bases_kernel(lon_ref, lat_ref, vals_lon, vals_lat, val_time, bases_hbm, vals_ref, bases, sems):
    lon, lat = lon_ref[...], lat_ref[...]
    copies = []
    for index, value in enumerate((lat.T, lon, lon.T, lat)):
        bases[index, 0], bases[index, 1] = halves(value)
        copies.append(
            pltpu.make_async_copy(bases.at[index], bases_hbm.at[index], sems.at[index])
        )
        copies[-1].start()
    vals_ref[0:1, :] = vals_lon[...]
    vals_ref[1:2, :] = vals_lat[...]
    vals_ref[2:3, :] = jnp.full((1, 512), val_time[0], F32)
    vals_ref[3:8, :] = jnp.zeros((5, 512), F32)
    for copy in copies:
        copy.wait()


def forward_kernel(
    obs_hbm, noise_hbm, prior_hbm, time_hbm, out_hbm, bufs, time, field, out_ref, sems, out_sems
):
    time_copy = pltpu.make_async_copy(time_hbm, time, sems.at[12])
    time_copy.start()
    copies = {}
    for source, j_half in ((0, 0), (1, 0), (0, 1), (1, 1), (2, 0), (2, 1)):
        array = (obs_hbm, noise_hbm, prior_hbm)[source]
        for k_half in range(2):
            slot = source * 4 + j_half * 2 + k_half
            copies[slot] = pltpu.make_async_copy(
                array.at[:, pl.ds(j_half * 8, 8), pl.ds(k_half * 128, 128)],
                bufs.at[slot],
                sems.at[slot],
            )
            copies[slot].start()
    time_copy.wait()
    basis = halves(time[...].T)

    sends = []

    def send(part):
        rows = pl.ds(part * 8, 8)
        copy = pltpu.make_async_copy(
            out_ref.reshape(256, 24, 128).at[:, rows, :], out_hbm.at[:, rows, :], out_sems.at[part]
        )
        copy.start()
        sends.append(copy)

    def rows(slot, jj):
        return bufs.at[slot].reshape(512, 128)[pl.ds(jj, 64, stride=8), :]

    for j_half in range(2):
        for k_half in range(2):
            copies[j_half * 2 + k_half].wait()
            copies[4 + j_half * 2 + k_half].wait()
        for jj in range(8):
            for k_half in range(2):
                obs = rows(j_half * 2 + k_half, jj)
                shifted = obs - NOISE_STD * rows(4 + j_half * 2 + k_half, jj)
                lanes = slice(k_half * 128, (k_half + 1) * 128)
                for f, value in enumerate((obs, shifted)):
                    target = slice(jj * 128 + f * 64, jj * 128 + (f + 1) * 64)
                    high, low = halves(value)
                    field[0, target, lanes] = high
                    field[1, target, lanes] = low
        result = product(basis, (field[0], field[1]), NT)
        for jj in range(8):
            out_ref[pl.ds(j_half * 8 + jj, 256, stride=24), :] = result[:, jj * 128:(jj + 1) * 128]
        send(j_half)

    for slot in range(8, 12):
        copies[slot].wait()
    for jj in range(8):
        for k_half in range(2):
            both = jnp.concatenate([rows(8 + k_half, jj), rows(10 + k_half, jj)], axis=0)
            out_ref[pl.ds(k_half * 3072 + 16 + jj, 128, stride=24), :] = both.T
    send(2)
    for copy in sends:
        copy.wait()


def middle_kernel(
    in_ref, bases_hbm, vals_hbm, out_ref, bases, vals, x_ref, y_ref, prior_ref, sems
):
    copies = [pltpu.make_async_copy(vals_hbm, vals, sems.at[4])]
    for index in range(4):
        copies.append(pltpu.make_async_copy(bases_hbm.at[index], bases.at[index], sems.at[index]))
    for copy in copies:
        copy.start()

    for p in range(4):
        def gather(blk, carry):
            rows = pl.ds(pl.multiple_of(blk * 128, 128), 128)
            even = pl.ds(p * 64 + blk * 8, 8)
            odd = pl.ds(p * 64 + 32 + blk * 8, 8)
            pair = interleave(
                in_ref[even, 0:16, :].reshape(128, 128), in_ref[odd, 0:16, :].reshape(128, 128)
            )
            for f in range(2):
                high, low = halves(pair[f])
                x_ref[0, rows, f * 512 + p * 128:f * 512 + (p + 1) * 128] = high
                x_ref[1, rows, f * 512 + p * 128:f * 512 + (p + 1) * 128] = low
            first, second = interleave(
                in_ref[even, 16:24, :].reshape(64, 128), in_ref[odd, 16:24, :].reshape(64, 128)
            )
            both = jnp.concatenate([first.reshape(8, 8, 128), second.reshape(8, 8, 128)], axis=1)
            prior_ref[rows, p * 128:(p + 1) * 128] = both.reshape(128, 128)
            return carry

        lax.fori_loop(0, 4, gather, 0)

    for copy in copies[:2]:
        copy.wait()
    result = product((bases[0, 0], bases[0, 1]), (x_ref[0], x_ref[1]), NN)
    for f in range(2):
        rows = slice(f * 512, (f + 1) * 512)
        y_ref[0, rows, :], y_ref[1, rows, :] = halves(result[:, f * 512:(f + 1) * 512])

    copies[2].wait()
    hat = product((y_ref[0], y_ref[1]), (bases[1, 0], bases[1, 1]), NN)
    spectrum = vals[0:1, :] * jnp.broadcast_to(vals[1:2, :], (512, 512)).T * vals[2:3, :]
    inverse = 1.0 / (spectrum + NOISE_VAR)
    y_ref[0, 0:512, :], y_ref[1, 0:512, :] = halves(hat[0:512] * inverse)
    y_ref[0, 512:1024, :], y_ref[1, 512:1024, :] = halves(
        jnp.sqrt(spectrum) * NOISE_VAR * inverse * prior_ref[...] + spectrum * inverse * hat[512:1024]
    )

    copies[3].wait()
    result = product((y_ref[0], y_ref[1]), (bases[2, 0], bases[2, 1]), NN)
    for f in range(2):
        lanes = slice(f * 512, (f + 1) * 512)
        x_ref[0, :, lanes], x_ref[1, :, lanes] = halves(result[f * 512:(f + 1) * 512])

    copies[4].wait()
    result = product((bases[3, 0], bases[3, 1]), (x_ref[0], x_ref[1]), NN)
    for p in range(4):
        even, odd = interleave(
            result[:, p * 128:(p + 1) * 128], result[:, 512 + p * 128:512 + (p + 1) * 128]
        )
        out_ref[p * 64:p * 64 + 32] = even.reshape(32, 16, 128)
        out_ref[p * 64 + 32:p * 64 + 64] = odd.reshape(32, 16, 128)


def backward_kernel(in_ref, time_ref, weights_hbm, sample_hbm, field, bufs, sems):
    basis = halves(time_ref[...])
    copies = []
    for j_half in range(2):
        for jj in range(8):
            lanes = slice(jj * 128, (jj + 1) * 128)
            high, low = halves(in_ref[pl.ds(j_half * 8 + jj, 256, stride=16), :])
            field[0, :, lanes] = high
            field[1, :, lanes] = low
        for k_half in range(2):
            left = tuple(half[k_half * 128:(k_half + 1) * 128] for half in basis)
            result = product(left, (field[0], field[1]), NN)
            slots = [f * 4 + j_half * 2 + k_half for f in range(2)]
            for jj in range(8):
                block = result[:, jj * 128:(jj + 1) * 128].T
                for f in range(2):
                    target = bufs.at[slots[f]].reshape(512, 128)
                    target[pl.ds(jj, 64, stride=8), :] = block[f * 64:(f + 1) * 64]
            for f, array in enumerate((weights_hbm, sample_hbm)):
                copy = pltpu.make_async_copy(
                    bufs.at[slots[f]],
                    array.at[:, pl.ds(j_half * 8, 8), pl.ds(k_half * 128, 128)],
                    sems.at[slots[f]],
                )
                copy.start()
                copies.append(copy)
    for copy in copies:
        copy.wait()


def shape(dims, kind=F32):
    return jax.ShapeDtypeStruct(dims, kind)


def cost(flops, nbytes):
    return pl.CostEstimate(flops=int(flops), bytes_accessed=int(nbytes), transcendentals=0)


def on_device(
    observed, prior_draw, noise_draw, basis_lon, basis_lat, basis_time, eig_lon, eig_lat, eig_time
):
    index = lax.axis_index("lon") * 32 + lax.axis_index("lat")
    val_time = lax.dynamic_slice_in_dim(eig_time, index, 1)

    bases, vals = pl.pallas_call(
        bases_kernel,
        out_shape=[shape((40, 2, 512, 512), BF16), shape((8, 512))],
        in_specs=[VMEM] * 4 + [SMEM],
        out_specs=[ANY, VMEM],
        scratch_shapes=[pltpu.VMEM((4, 2, 512, 512), BF16), pltpu.SemaphoreType.DMA((4,))],
        compiler_params=pltpu.CompilerParams(vmem_limit_bytes=32 * MIB),
        cost_estimate=cost(4 * MIB, 8 * MIB),
        name="bases",
    )(basis_lon, basis_lat, eig_lon.reshape(1, 512), eig_lat.reshape(1, 512), val_time)

    packed = pl.pallas_call(
        forward_kernel,
        out_shape=shape((256, 24, 128)),
        in_specs=[ANY] * 4,
        out_specs=ANY,
        scratch_shapes=[
            pltpu.VMEM((12, 64, 8, 128), F32),
            pltpu.VMEM((256, 256), F32),
            pltpu.VMEM((2, 1024, 256), BF16),
            pltpu.VMEM((6144, 128), F32),
            pltpu.SemaphoreType.DMA((13,)),
            pltpu.SemaphoreType.DMA((3,)),
        ],
        compiler_params=pltpu.CompilerParams(vmem_limit_bytes=58 * MIB),
        cost_estimate=cost(3 * 2 * 2048 * 256 * 256, 6 * MIB),
        name="time_forward",
    )(observed, noise_draw, prior_draw, basis_time)
    packed = lax.all_to_all(packed, ("lon", "lat"), 0, 0, tiled=True)

    planes = pl.pallas_call(
        middle_kernel,
        out_shape=shape((256, 16, 128)),
        in_specs=[VMEM, ANY, ANY],
        out_specs=VMEM,
        scratch_shapes=[
            pltpu.VMEM((4, 2, 512, 512), BF16),
            pltpu.VMEM((8, 512), F32),
            pltpu.VMEM((2, 512, 1024), BF16),
            pltpu.VMEM((2, 1024, 512), BF16),
            pltpu.VMEM((512, 512), F32),
            pltpu.SemaphoreType.DMA((5,)),
        ],
        compiler_params=pltpu.CompilerParams(vmem_limit_bytes=32 * MIB),
        cost_estimate=cost(3 * 2 * 8 * 512**3, 8 * MIB),
        name="middle",
    )(packed, bases, vals)
    planes = lax.all_to_all(planes, ("lon", "lat"), 0, 0, tiled=True)

    weights, sample = pl.pallas_call(
        backward_kernel,
        out_shape=[shape((64, 16, 256))] * 2,
        in_specs=[VMEM] * 2,
        out_specs=[ANY] * 2,
        scratch_shapes=[
            pltpu.VMEM((2, 256, 1024), BF16),
            pltpu.VMEM((8, 64, 8, 128), F32),
            pltpu.SemaphoreType.DMA((8,)),
        ],
        compiler_params=pltpu.CompilerParams(vmem_limit_bytes=32 * MIB),
        cost_estimate=cost(3 * 2 * 2048 * 256 * 256, 4 * MIB),
        name="time_backward",
    )(planes.reshape(4096, 128), basis_time)
    return weights, sample


def solution(mesh):
    block = P("lon", "lat", None)
    return jax.shard_map(
        on_device,
        mesh=mesh,
        in_specs=(block,) * 3 + (P(),) * 6,
        out_specs=(block, block),
        check_vma=False,
    )
```

```python
import jax
import jax.numpy as jnp
from jax import lax
from jax.experimental import pallas as pl
from jax.experimental.pallas import tpu as pltpu
from jax.sharding import PartitionSpec as P

NOISE_VAR = 0.25
NOISE_STD = 0.5
BF16 = jnp.bfloat16
F32 = jnp.float32
MIB = 1 << 20
VMEM = pl.BlockSpec(memory_space=pltpu.VMEM)
SMEM = pl.BlockSpec(memory_space=pltpu.SMEM)
ANY = pl.BlockSpec(memory_space=pl.ANY)
NN = (((1,), (0,)), ((), ()))
NT = (((1,), (1,)), ((), ()))


def halves(value):
    high = value.astype(BF16)
    low = (value - high.astype(F32)).astype(BF16)
    return high, low


def product(left, right, dims=NN):
    depth = dims[0][1][0]
    return lax.dot_general(
        jnp.concatenate([left[0], left[0], left[1]], axis=1),
        jnp.concatenate([right[0], right[1], right[0]], axis=depth),
        dimension_numbers=dims,
        preferred_element_type=F32,
    )


def interleave(first, second):
    lanes = lax.broadcasted_iota(jnp.int32, first.shape, 1)
    lower = lanes < 64
    return (
        jnp.where(lower, first, pltpu.roll(second, 64, 1)),
        jnp.where(lower, pltpu.roll(first, 64, 1), second),
    )


def bases_kernel(
    lon_ref, lat_ref, vals_lon, vals_lat, val_time, bases_hbm, scales_hbm, bases, scales, sems
):
    lon, lat = lon_ref[...], lat_ref[...]
    copies = []
    for index, value in enumerate((lat.T, lon, lon.T, lat)):
        bases[index, 0], bases[index, 1] = halves(value)
        copies.append(
            pltpu.make_async_copy(bases.at[index], bases_hbm.at[index], sems.at[index])
        )
        copies[-1].start()
    column = jnp.broadcast_to(vals_lat[...], (512, 512)).T
    spectrum = vals_lon[...] * column * val_time[0]
    inverse = 1.0 / (spectrum + NOISE_VAR)
    scales[0] = inverse
    scales[1] = jnp.sqrt(spectrum) * NOISE_VAR * inverse
    scales[2] = spectrum * inverse
    copies.append(pltpu.make_async_copy(scales, scales_hbm.at[0:3], sems.at[4]))
    copies[-1].start()
    for copy in copies:
        copy.wait()


def forward_kernel(
    obs_hbm, noise_hbm, prior_hbm, time_hbm, out_hbm, bufs, time, field, out_ref, sems, out_sems
):
    time_copy = pltpu.make_async_copy(time_hbm, time, sems.at[12])
    time_copy.start()
    copies = {}
    for source, j_half in ((0, 0), (1, 0), (0, 1), (1, 1), (2, 0), (2, 1)):
        array = (obs_hbm, noise_hbm, prior_hbm)[source]
        for k_half in range(2):
            slot = source * 4 + j_half * 2 + k_half
            copies[slot] = pltpu.make_async_copy(
                array.at[:, pl.ds(j_half * 8, 8), pl.ds(k_half * 128, 128)],
                bufs.at[slot],
                sems.at[slot],
            )
            copies[slot].start()
    time_copy.wait()
    basis = halves(time[...].T)

    sends = []

    def send(part):
        rows = pl.ds(part * 8, 8)
        copy = pltpu.make_async_copy(
            out_ref.reshape(256, 24, 128).at[:, rows, :], out_hbm.at[:, rows, :], out_sems.at[part]
        )
        copy.start()
        sends.append(copy)

    def rows(slot, jj):
        return bufs.at[slot].reshape(512, 128)[pl.ds(jj, 64, stride=8), :]

    for j_half in range(2):
        for k_half in range(2):
            copies[j_half * 2 + k_half].wait()
            copies[4 + j_half * 2 + k_half].wait()
        for jj in range(8):
            for k_half in range(2):
                obs = rows(j_half * 2 + k_half, jj)
                shifted = obs - NOISE_STD * rows(4 + j_half * 2 + k_half, jj)
                lanes = slice(k_half * 128, (k_half + 1) * 128)
                for f, value in enumerate((obs, shifted)):
                    target = slice(jj * 128 + f * 64, jj * 128 + (f + 1) * 64)
                    high, low = halves(value)
                    field[0, target, lanes] = high
                    field[1, target, lanes] = low
        result = product(basis, (field[0], field[1]), NT)
        for jj in range(8):
            out_ref[pl.ds(j_half * 8 + jj, 256, stride=24), :] = result[:, jj * 128:(jj + 1) * 128]
        send(j_half)

    for slot in range(8, 12):
        copies[slot].wait()
    for jj in range(8):
        for k_half in range(2):
            both = jnp.concatenate([rows(8 + k_half, jj), rows(10 + k_half, jj)], axis=0)
            out_ref[pl.ds(k_half * 3072 + 16 + jj, 128, stride=24), :] = both.T
    send(2)
    for copy in sends:
        copy.wait()


def middle_kernel(
    in_ref, bases_hbm, scales_hbm, out_ref, bases, scales, x_ref, y_ref, prior_ref, sems
):
    copies = [
        pltpu.make_async_copy(bases_hbm.at[index], bases.at[index], sems.at[index])
        for index in range(4)
    ]
    copies.insert(2, pltpu.make_async_copy(scales_hbm.at[0:3], scales, sems.at[4]))
    for copy in copies:
        copy.start()
    latt, lon, lont, lat = ((bases.at[index, 0], bases.at[index, 1]) for index in range(4))
    fields = (slice(0, 512), slice(512, 1024))

    def split(ref):
        return (ref[0][...], ref[1][...])

    for p in range(4):
        lanes = slice(p * 128, (p + 1) * 128)
        for block in range(4):
            rows = slice(block * 128, (block + 1) * 128)
            even = slice(p * 64 + block * 8, p * 64 + block * 8 + 8)
            odd = slice(p * 64 + 32 + block * 8, p * 64 + 32 + block * 8 + 8)
            pair = interleave(
                in_ref[even, 0:16, :].reshape(128, 128), in_ref[odd, 0:16, :].reshape(128, 128)
            )
            for f in range(2):
                target = slice(f * 512 + p * 128, f * 512 + (p + 1) * 128)
                x_ref[0, rows, target], x_ref[1, rows, target] = halves(pair[f])
            first, second = interleave(
                in_ref[even, 16:24, :].reshape(64, 128), in_ref[odd, 16:24, :].reshape(64, 128)
            )
            both = jnp.concatenate([first.reshape(8, 8, 128), second.reshape(8, 8, 128)], axis=1)
            prior_ref[rows, lanes] = both.reshape(128, 128)

    copies[0].wait()
    result = product(split(latt), (x_ref[0], x_ref[1]))
    for rows in fields:
        y_ref[0, rows, :], y_ref[1, rows, :] = halves(result[:, rows])

    copies[1].wait()
    copies[2].wait()
    hat = product((y_ref[0], y_ref[1]), split(lon))
    weight_hat = hat[fields[0]] * scales[0]
    sample_hat = scales[1] * prior_ref[...] + scales[2] * hat[fields[1]]
    for rows, value in zip(fields, (weight_hat, sample_hat)):
        y_ref[0, rows, :], y_ref[1, rows, :] = halves(value)

    copies[3].wait()
    result = product((y_ref[0], y_ref[1]), split(lont))
    for rows in fields:
        x_ref[0, :, rows], x_ref[1, :, rows] = halves(result[rows])

    copies[4].wait()
    result = product(split(lat), (x_ref[0], x_ref[1]))
    for p in range(4):
        even, odd = interleave(
            result[:, p * 128:(p + 1) * 128], result[:, 512 + p * 128:512 + (p + 1) * 128]
        )
        out_ref[p * 64:p * 64 + 32] = even.reshape(32, 16, 128)
        out_ref[p * 64 + 32:p * 64 + 64] = odd.reshape(32, 16, 128)


def backward_kernel(in_ref, time_ref, weights_hbm, sample_hbm, field, bufs, sems):
    basis = halves(time_ref[...])
    copies = []
    for j_half in range(2):
        for jj in range(8):
            lanes = slice(jj * 128, (jj + 1) * 128)
            high, low = halves(in_ref[pl.ds(j_half * 8 + jj, 256, stride=16), :])
            field[0, :, lanes] = high
            field[1, :, lanes] = low
        for k_half in range(2):
            left = tuple(half[k_half * 128:(k_half + 1) * 128] for half in basis)
            result = product(left, (field[0], field[1]))
            slots = [f * 4 + j_half * 2 + k_half for f in range(2)]
            for jj in range(8):
                block = result[:, jj * 128:(jj + 1) * 128].T
                for f in range(2):
                    target = bufs.at[slots[f]].reshape(512, 128)
                    target[pl.ds(jj, 64, stride=8), :] = block[f * 64:(f + 1) * 64]
            for f, array in enumerate((weights_hbm, sample_hbm)):
                copy = pltpu.make_async_copy(
                    bufs.at[slots[f]],
                    array.at[:, pl.ds(j_half * 8, 8), pl.ds(k_half * 128, 128)],
                    sems.at[slots[f]],
                )
                copy.start()
                copies.append(copy)
    for copy in copies:
        copy.wait()


def shape(dims, kind=F32):
    return jax.ShapeDtypeStruct(dims, kind)


def cost(flops, nbytes):
    return pl.CostEstimate(flops=int(flops), bytes_accessed=int(nbytes), transcendentals=0)


def on_device(
    observed, prior_draw, noise_draw, basis_lon, basis_lat, basis_time, eig_lon, eig_lat, eig_time
):
    index = lax.axis_index("lon") * 32 + lax.axis_index("lat")
    val_time = lax.dynamic_slice_in_dim(eig_time, index, 1)

    bases, scales = pl.pallas_call(
        bases_kernel,
        out_shape=[shape((40, 2, 512, 512), BF16), shape((40, 512, 512))],
        in_specs=[VMEM] * 4 + [SMEM],
        out_specs=[ANY, ANY],
        scratch_shapes=[
            pltpu.VMEM((4, 2, 512, 512), BF16),
            pltpu.VMEM((3, 512, 512), F32),
            pltpu.SemaphoreType.DMA((5,)),
        ],
        compiler_params=pltpu.CompilerParams(vmem_limit_bytes=32 * MIB),
        cost_estimate=cost(4 * MIB, 8 * MIB),
        name="bases",
    )(basis_lon, basis_lat, eig_lon.reshape(1, 512), eig_lat.reshape(1, 512), val_time)

    packed = pl.pallas_call(
        forward_kernel,
        out_shape=shape((256, 24, 128)),
        in_specs=[ANY] * 4,
        out_specs=ANY,
        scratch_shapes=[
            pltpu.VMEM((12, 64, 8, 128), F32),
            pltpu.VMEM((256, 256), F32),
            pltpu.VMEM((2, 1024, 256), BF16),
            pltpu.VMEM((6144, 128), F32),
            pltpu.SemaphoreType.DMA((13,)),
            pltpu.SemaphoreType.DMA((3,)),
        ],
        compiler_params=pltpu.CompilerParams(vmem_limit_bytes=58 * MIB),
        cost_estimate=cost(3 * 2 * 2048 * 256 * 256, 6 * MIB),
        name="time_forward",
    )(observed, noise_draw, prior_draw, basis_time)
    packed = lax.all_to_all(packed, ("lon", "lat"), 0, 0, tiled=True)

    planes = pl.pallas_call(
        middle_kernel,
        out_shape=shape((256, 16, 128)),
        in_specs=[VMEM, ANY, ANY],
        out_specs=VMEM,
        scratch_shapes=[
            pltpu.VMEM((4, 2, 512, 512), BF16),
            pltpu.VMEM((3, 512, 512), F32),
            pltpu.VMEM((2, 512, 1024), BF16),
            pltpu.VMEM((2, 1024, 512), BF16),
            pltpu.VMEM((512, 512), F32),
            pltpu.SemaphoreType.DMA((5,)),
        ],
        compiler_params=pltpu.CompilerParams(vmem_limit_bytes=32 * MIB),
        cost_estimate=cost(3 * 2 * 8 * 512**3, 8 * MIB),
        name="middle",
    )(packed, bases, scales)
    planes = lax.all_to_all(planes, ("lon", "lat"), 0, 0, tiled=True)

    weights, sample = pl.pallas_call(
        backward_kernel,
        out_shape=[shape((64, 16, 256))] * 2,
        in_specs=[VMEM] * 2,
        out_specs=[ANY] * 2,
        scratch_shapes=[
            pltpu.VMEM((2, 256, 1024), BF16),
            pltpu.VMEM((8, 64, 8, 128), F32),
            pltpu.SemaphoreType.DMA((8,)),
        ],
        compiler_params=pltpu.CompilerParams(vmem_limit_bytes=32 * MIB),
        cost_estimate=cost(3 * 2 * 2048 * 256 * 256, 4 * MIB),
        name="time_backward",
    )(planes.reshape(4096, 128), basis_time)
    return weights, sample


def solution(mesh):
    block = P("lon", "lat", None)
    return jax.shard_map(
        on_device,
        mesh=mesh,
        in_specs=(block,) * 3 + (P(),) * 6,
        out_specs=(block, block),
        check_vma=False,
    )
```

```python
import jax
import jax.numpy as jnp
from jax import lax
from jax.experimental import pallas as pl
from jax.experimental.pallas import tpu as pltpu
from jax.sharding import PartitionSpec as P

NOISE_VAR = 0.25
NOISE_STD = 0.5
BF16 = jnp.bfloat16
F32 = jnp.float32
MIB = 1 << 20
VMEM = pl.BlockSpec(memory_space=pltpu.VMEM)
SMEM = pl.BlockSpec(memory_space=pltpu.SMEM)
ANY = pl.BlockSpec(memory_space=pl.ANY)
NN = (((1,), (0,)), ((), ()))
NT = (((1,), (1,)), ((), ()))


def halves(value):
    high = value.astype(BF16)
    low = (value - high.astype(F32)).astype(BF16)
    return high, low


def product(left, right, dims=NN):
    depth = dims[0][1][0]
    return lax.dot_general(
        jnp.concatenate([left[0], left[0], left[1]], axis=1),
        jnp.concatenate([right[0], right[1], right[0]], axis=depth),
        dimension_numbers=dims,
        preferred_element_type=F32,
    )


def interleave(first, second):
    lanes = lax.broadcasted_iota(jnp.int32, first.shape, 1)
    lower = lanes < 64
    return (
        jnp.where(lower, first, pltpu.roll(second, 64, 1)),
        jnp.where(lower, pltpu.roll(first, 64, 1), second),
    )


def forward_kernel(
    obs_hbm, noise_hbm, prior_hbm, time_hbm, out_hbm, bufs, time, field, out_ref, sems, out_sems
):
    time_copy = pltpu.make_async_copy(time_hbm, time, sems.at[12])
    time_copy.start()
    copies = {}
    for source, j_half in ((0, 0), (1, 0), (0, 1), (1, 1), (2, 0), (2, 1)):
        array = (obs_hbm, noise_hbm, prior_hbm)[source]
        for k_half in range(2):
            slot = source * 4 + j_half * 2 + k_half
            copies[slot] = pltpu.make_async_copy(
                array.at[:, pl.ds(j_half * 8, 8), pl.ds(k_half * 128, 128)],
                bufs.at[slot],
                sems.at[slot],
            )
            copies[slot].start()
    time_copy.wait()
    basis = halves(time[...].T)

    sends = []

    def send(part):
        rows = pl.ds(part * 8, 8)
        copy = pltpu.make_async_copy(
            out_ref.reshape(256, 24, 128).at[:, rows, :], out_hbm.at[:, rows, :], out_sems.at[part]
        )
        copy.start()
        sends.append(copy)

    def rows(slot, jj):
        return bufs.at[slot].reshape(512, 128)[pl.ds(jj, 64, stride=8), :]

    for j_half in range(2):
        for k_half in range(2):
            copies[j_half * 2 + k_half].wait()
            copies[4 + j_half * 2 + k_half].wait()
        for jj in range(8):
            for k_half in range(2):
                obs = rows(j_half * 2 + k_half, jj)
                shifted = obs - NOISE_STD * rows(4 + j_half * 2 + k_half, jj)
                lanes = slice(k_half * 128, (k_half + 1) * 128)
                for f, value in enumerate((obs, shifted)):
                    target = slice(jj * 128 + f * 64, jj * 128 + (f + 1) * 64)
                    high, low = halves(value)
                    field[0, target, lanes] = high
                    field[1, target, lanes] = low
        result = product(basis, (field[0], field[1]), NT)
        for jj in range(8):
            out_ref[pl.ds(j_half * 8 + jj, 256, stride=24), :] = result[:, jj * 128:(jj + 1) * 128]
        send(j_half)

    for slot in range(8, 12):
        copies[slot].wait()
    for jj in range(8):
        for k_half in range(2):
            both = jnp.concatenate([rows(8 + k_half, jj), rows(10 + k_half, jj)], axis=0)
            out_ref[pl.ds(k_half * 3072 + 16 + jj, 128, stride=24), :] = both.T
    send(2)
    for copy in sends:
        copy.wait()


def middle_kernel(
    in_ref, lon_ref, lat_ref, vals_lon, vals_lat, vals_time, out_ref, x_ref, y_ref, prior_ref
):
    latt = halves(lat_ref[...].T)
    fields = (slice(0, 512), slice(512, 1024))

    for p in range(4):
        lanes = slice(p * 128, (p + 1) * 128)
        for block in range(4):
            rows = slice(block * 128, (block + 1) * 128)
            even = slice(p * 64 + block * 8, p * 64 + block * 8 + 8)
            odd = slice(p * 64 + 32 + block * 8, p * 64 + 32 + block * 8 + 8)
            pair = interleave(
                in_ref[even, 0:16, :].reshape(128, 128), in_ref[odd, 0:16, :].reshape(128, 128)
            )
            for f in range(2):
                target = slice(f * 512 + p * 128, f * 512 + (p + 1) * 128)
                x_ref[0, rows, target], x_ref[1, rows, target] = halves(pair[f])
            first, second = interleave(
                in_ref[even, 16:24, :].reshape(64, 128), in_ref[odd, 16:24, :].reshape(64, 128)
            )
            both = jnp.concatenate([first.reshape(8, 8, 128), second.reshape(8, 8, 128)], axis=1)
            prior_ref[rows, lanes] = both.reshape(128, 128)

    result = product(latt, (x_ref[0], x_ref[1]))
    for rows in fields:
        y_ref[0, rows, :], y_ref[1, rows, :] = halves(result[:, rows])

    lon = halves(lon_ref[...])
    hat = product((y_ref[0], y_ref[1]), lon)
    index = lax.axis_index("lon") * 32 + lax.axis_index("lat")
    column = jnp.broadcast_to(vals_lat[...], (512, 512)).T
    spectrum = vals_lon[...] * column * vals_time[index]
    inverse = 1.0 / (spectrum + NOISE_VAR)
    weight_hat = hat[fields[0]] * inverse
    prior_scale = jnp.sqrt(spectrum) * NOISE_VAR * inverse
    sample_hat = prior_scale * prior_ref[...] + spectrum * inverse * hat[fields[1]]
    for rows, value in zip(fields, (weight_hat, sample_hat)):
        y_ref[0, rows, :], y_ref[1, rows, :] = halves(value)

    result = product((y_ref[0], y_ref[1]), lon, NT)
    for rows in fields:
        x_ref[0, :, rows], x_ref[1, :, rows] = halves(result[rows])

    result = product(halves(lat_ref[...]), (x_ref[0], x_ref[1]))
    for p in range(4):
        even, odd = interleave(
            result[:, p * 128:(p + 1) * 128], result[:, 512 + p * 128:512 + (p + 1) * 128]
        )
        out_ref[p * 64:p * 64 + 32] = even.reshape(32, 16, 128)
        out_ref[p * 64 + 32:p * 64 + 64] = odd.reshape(32, 16, 128)


def backward_kernel(in_ref, time_ref, weights_hbm, sample_hbm, field, bufs, sems):
    basis = halves(time_ref[...])
    copies = []
    for j_half in range(2):
        for jj in range(8):
            lanes = slice(jj * 128, (jj + 1) * 128)
            high, low = halves(in_ref[pl.ds(j_half * 8 + jj, 256, stride=16), :])
            field[0, :, lanes] = high
            field[1, :, lanes] = low
        for k_half in range(2):
            left = tuple(half[k_half * 128:(k_half + 1) * 128] for half in basis)
            result = product(left, (field[0], field[1]))
            slots = [f * 4 + j_half * 2 + k_half for f in range(2)]
            for jj in range(8):
                block = result[:, jj * 128:(jj + 1) * 128].T
                for f in range(2):
                    target = bufs.at[slots[f]].reshape(512, 128)
                    target[pl.ds(jj, 64, stride=8), :] = block[f * 64:(f + 1) * 64]
            for f, array in enumerate((weights_hbm, sample_hbm)):
                copy = pltpu.make_async_copy(
                    bufs.at[slots[f]],
                    array.at[:, pl.ds(j_half * 8, 8), pl.ds(k_half * 128, 128)],
                    sems.at[slots[f]],
                )
                copy.start()
                copies.append(copy)
    for copy in copies:
        copy.wait()


def shape(dims, kind=F32):
    return jax.ShapeDtypeStruct(dims, kind)


def cost(flops, nbytes):
    return pl.CostEstimate(flops=int(flops), bytes_accessed=int(nbytes), transcendentals=0)


def on_device(
    observed, prior_draw, noise_draw, basis_lon, basis_lat, basis_time, eig_lon, eig_lat, eig_time
):
    packed = pl.pallas_call(
        forward_kernel,
        out_shape=shape((256, 24, 128)),
        in_specs=[ANY] * 4,
        out_specs=ANY,
        scratch_shapes=[
            pltpu.VMEM((12, 64, 8, 128), F32),
            pltpu.VMEM((256, 256), F32),
            pltpu.VMEM((2, 1024, 256), BF16),
            pltpu.VMEM((6144, 128), F32),
            pltpu.SemaphoreType.DMA((13,)),
            pltpu.SemaphoreType.DMA((3,)),
        ],
        compiler_params=pltpu.CompilerParams(vmem_limit_bytes=58 * MIB),
        cost_estimate=cost(3 * 2 * 2048 * 256 * 256, 6 * MIB),
        name="time_forward",
    )(observed, noise_draw, prior_draw, basis_time)
    packed = lax.all_to_all(packed, ("lon", "lat"), 0, 0, tiled=True)

    planes = pl.pallas_call(
        middle_kernel,
        out_shape=shape((256, 16, 128)),
        in_specs=[VMEM] * 5 + [SMEM],
        out_specs=VMEM,
        scratch_shapes=[
            pltpu.VMEM((2, 512, 1024), BF16),
            pltpu.VMEM((2, 1024, 512), BF16),
            pltpu.VMEM((512, 512), F32),
        ],
        compiler_params=pltpu.CompilerParams(vmem_limit_bytes=32 * MIB),
        cost_estimate=cost(3 * 2 * 8 * 512**3, 8 * MIB),
        name="middle",
    )(
        packed,
        basis_lon,
        basis_lat,
        eig_lon.reshape(1, 512),
        eig_lat.reshape(1, 512),
        eig_time,
    )
    planes = lax.all_to_all(planes, ("lon", "lat"), 0, 0, tiled=True)

    weights, sample = pl.pallas_call(
        backward_kernel,
        out_shape=[shape((64, 16, 256))] * 2,
        in_specs=[VMEM] * 2,
        out_specs=[ANY] * 2,
        scratch_shapes=[
            pltpu.VMEM((2, 256, 1024), BF16),
            pltpu.VMEM((8, 64, 8, 128), F32),
            pltpu.SemaphoreType.DMA((8,)),
        ],
        compiler_params=pltpu.CompilerParams(vmem_limit_bytes=32 * MIB),
        cost_estimate=cost(3 * 2 * 2048 * 256 * 256, 4 * MIB),
        name="time_backward",
    )(planes.reshape(4096, 128), basis_time)
    return weights, sample


def solution(mesh):
    block = P("lon", "lat", None)
    return jax.shard_map(
        on_device,
        mesh=mesh,
        in_specs=(block,) * 3 + (P(),) * 6,
        out_specs=(block, block),
        check_vma=False,
    )
```

```python
import jax
import jax.numpy as jnp
from jax import lax
from jax.experimental import pallas as pl
from jax.experimental.pallas import tpu as pltpu
from jax.sharding import PartitionSpec as P

NOISE_VAR = 0.25
NOISE_STD = 0.5
BF16 = jnp.bfloat16
F32 = jnp.float32
MIB = 1 << 20
VMEM = pl.BlockSpec(memory_space=pltpu.VMEM)
SMEM = pl.BlockSpec(memory_space=pltpu.SMEM)
ANY = pl.BlockSpec(memory_space=pl.ANY)
NN = (((1,), (0,)), ((), ()))
NT = (((1,), (1,)), ((), ()))


def halves(value):
    high = value.astype(BF16)
    low = (value - high.astype(F32)).astype(BF16)
    return high, low


def product(left, right, dims=NN):
    depth = dims[0][1][0]
    return lax.dot_general(
        jnp.concatenate([left[0], left[0], left[1]], axis=1),
        jnp.concatenate([right[0], right[1], right[0]], axis=depth),
        dimension_numbers=dims,
        preferred_element_type=F32,
    )


def interleave(first, second):
    lanes = lax.broadcasted_iota(jnp.int32, first.shape, 1)
    lower = lanes < 64
    return (
        jnp.where(lower, first, pltpu.roll(second, 64, 1)),
        jnp.where(lower, pltpu.roll(first, 64, 1), second),
    )


def forward_kernel(
    obs_hbm, noise_hbm, prior_hbm, time_hbm, out_hbm, bufs, time, field, out_ref, sems, out_sems
):
    time_copy = pltpu.make_async_copy(time_hbm, time, sems.at[12])
    time_copy.start()
    copies = {}
    for source, j_half in ((0, 0), (1, 0), (0, 1), (1, 1), (2, 0), (2, 1)):
        array = (obs_hbm, noise_hbm, prior_hbm)[source]
        for k_half in range(2):
            slot = source * 4 + j_half * 2 + k_half
            copies[slot] = pltpu.make_async_copy(
                array.at[:, pl.ds(j_half * 8, 8), pl.ds(k_half * 128, 128)],
                bufs.at[slot],
                sems.at[slot],
            )
            copies[slot].start()
    time_copy.wait()
    basis = halves(time[...].T)

    sends = []

    def send(part, first=0, count=256, sem=None):
        steps, rows = pl.ds(first, count), pl.ds(part * 8, 8)
        copy = pltpu.make_async_copy(
            out_ref.reshape(256, 24, 128).at[steps, rows, :],
            out_hbm.at[steps, rows, :],
            out_sems.at[part if sem is None else sem],
        )
        copy.start()
        sends.append(copy)

    def rows(slot, jj):
        return bufs.at[slot].reshape(512, 128)[pl.ds(jj, 64, stride=8), :]

    for j_half in range(2):
        for k_half in range(2):
            copies[j_half * 2 + k_half].wait()
            copies[4 + j_half * 2 + k_half].wait()
        for jj in range(8):
            for k_half in range(2):
                obs = rows(j_half * 2 + k_half, jj)
                shifted = obs - NOISE_STD * rows(4 + j_half * 2 + k_half, jj)
                lanes = slice(k_half * 128, (k_half + 1) * 128)
                for f, value in enumerate((obs, shifted)):
                    target = slice(jj * 128 + f * 64, jj * 128 + (f + 1) * 64)
                    high, low = halves(value)
                    field[0, target, lanes] = high
                    field[1, target, lanes] = low
        result = product(basis, (field[0], field[1]), NT)
        for jj in range(8):
            out_ref[pl.ds(j_half * 8 + jj, 256, stride=24), :] = result[:, jj * 128:(jj + 1) * 128]
        send(j_half)

    for slot in range(8, 12):
        copies[slot].wait()
    for k_half in range(2):
        for jj in range(8):
            both = jnp.concatenate([rows(8 + k_half, jj), rows(10 + k_half, jj)], axis=0)
            out_ref[pl.ds(k_half * 3072 + 16 + jj, 128, stride=24), :] = both.T
        send(2, k_half * 128, 128, 2 + k_half)
    for copy in sends:
        copy.wait()


def middle_kernel(
    in_ref, lon_ref, lat_ref, vals_lon, vals_lat, vals_time, out_ref, x_ref, y_ref, prior_ref
):
    latt = halves(lat_ref[...].T)
    fields = (slice(0, 512), slice(512, 1024))

    for p in range(4):
        lanes = slice(p * 128, (p + 1) * 128)
        for block in range(4):
            rows = slice(block * 128, (block + 1) * 128)
            even = slice(p * 64 + block * 8, p * 64 + block * 8 + 8)
            odd = slice(p * 64 + 32 + block * 8, p * 64 + 32 + block * 8 + 8)
            pair = interleave(
                in_ref[even, 0:16, :].reshape(128, 128), in_ref[odd, 0:16, :].reshape(128, 128)
            )
            for f in range(2):
                target = slice(f * 512 + p * 128, f * 512 + (p + 1) * 128)
                x_ref[0, rows, target], x_ref[1, rows, target] = halves(pair[f])
            first, second = interleave(
                in_ref[even, 16:24, :].reshape(64, 128), in_ref[odd, 16:24, :].reshape(64, 128)
            )
            both = jnp.concatenate([first.reshape(8, 8, 128), second.reshape(8, 8, 128)], axis=1)
            prior_ref[rows, lanes] = both.reshape(128, 128)

    result = product(latt, (x_ref[0], x_ref[1]))
    for rows in fields:
        y_ref[0, rows, :], y_ref[1, rows, :] = halves(result[:, rows])

    lon = halves(lon_ref[...])
    hat = product((y_ref[0], y_ref[1]), lon)
    index = lax.axis_index("lon") * 32 + lax.axis_index("lat")
    column = jnp.broadcast_to(vals_lat[...], (512, 512)).T
    spectrum = vals_lon[...] * column * vals_time[index]
    inverse = 1.0 / (spectrum + NOISE_VAR)
    weight_hat = hat[fields[0]] * inverse
    prior_scale = jnp.sqrt(spectrum) * NOISE_VAR * inverse
    sample_hat = prior_scale * prior_ref[...] + spectrum * inverse * hat[fields[1]]
    for rows, value in zip(fields, (weight_hat, sample_hat)):
        y_ref[0, rows, :], y_ref[1, rows, :] = halves(value)

    result = product((y_ref[0], y_ref[1]), lon, NT)
    for rows in fields:
        x_ref[0, :, rows], x_ref[1, :, rows] = halves(result[rows])

    result = product(halves(lat_ref[...]), (x_ref[0], x_ref[1]))
    for p in range(4):
        even, odd = interleave(
            result[:, p * 128:(p + 1) * 128], result[:, 512 + p * 128:512 + (p + 1) * 128]
        )
        out_ref[p * 64:p * 64 + 32] = even.reshape(32, 16, 128)
        out_ref[p * 64 + 32:p * 64 + 64] = odd.reshape(32, 16, 128)


def backward_kernel(in_ref, time_ref, weights_hbm, sample_hbm, field, bufs, sems):
    basis = halves(time_ref[...])
    copies = []
    for j_half in range(2):
        for jj in range(8):
            lanes = slice(jj * 128, (jj + 1) * 128)
            high, low = halves(in_ref[pl.ds(j_half * 8 + jj, 256, stride=16), :])
            field[0, :, lanes] = high
            field[1, :, lanes] = low
        for k_half in range(2):
            left = tuple(half[k_half * 128:(k_half + 1) * 128] for half in basis)
            result = product(left, (field[0], field[1]))
            slots = [f * 4 + j_half * 2 + k_half for f in range(2)]
            for jj in range(8):
                block = result[:, jj * 128:(jj + 1) * 128].T
                for f in range(2):
                    target = bufs.at[slots[f]].reshape(512, 128)
                    target[pl.ds(jj, 64, stride=8), :] = block[f * 64:(f + 1) * 64]
            for f, array in enumerate((weights_hbm, sample_hbm)):
                copy = pltpu.make_async_copy(
                    bufs.at[slots[f]],
                    array.at[:, pl.ds(j_half * 8, 8), pl.ds(k_half * 128, 128)],
                    sems.at[slots[f]],
                )
                copy.start()
                copies.append(copy)
    for copy in copies:
        copy.wait()


def shape(dims, kind=F32):
    return jax.ShapeDtypeStruct(dims, kind)


def cost(flops, nbytes):
    return pl.CostEstimate(flops=int(flops), bytes_accessed=int(nbytes), transcendentals=0)


def on_device(
    observed, prior_draw, noise_draw, basis_lon, basis_lat, basis_time, eig_lon, eig_lat, eig_time
):
    packed = pl.pallas_call(
        forward_kernel,
        out_shape=shape((256, 24, 128)),
        in_specs=[ANY] * 4,
        out_specs=ANY,
        scratch_shapes=[
            pltpu.VMEM((12, 64, 8, 128), F32),
            pltpu.VMEM((256, 256), F32),
            pltpu.VMEM((2, 1024, 256), BF16),
            pltpu.VMEM((6144, 128), F32),
            pltpu.SemaphoreType.DMA((13,)),
            pltpu.SemaphoreType.DMA((4,)),
        ],
        compiler_params=pltpu.CompilerParams(vmem_limit_bytes=58 * MIB),
        cost_estimate=cost(3 * 2 * 2048 * 256 * 256, 6 * MIB),
        name="time_forward",
    )(observed, noise_draw, prior_draw, basis_time)
    packed = lax.all_to_all(packed, ("lon", "lat"), 0, 0, tiled=True)

    planes = pl.pallas_call(
        middle_kernel,
        out_shape=shape((256, 16, 128)),
        in_specs=[VMEM] * 5 + [SMEM],
        out_specs=VMEM,
        scratch_shapes=[
            pltpu.VMEM((2, 512, 1024), BF16),
            pltpu.VMEM((2, 1024, 512), BF16),
            pltpu.VMEM((512, 512), F32),
        ],
        compiler_params=pltpu.CompilerParams(vmem_limit_bytes=32 * MIB),
        cost_estimate=cost(3 * 2 * 8 * 512**3, 8 * MIB),
        name="middle",
    )(
        packed,
        basis_lon,
        basis_lat,
        eig_lon.reshape(1, 512),
        eig_lat.reshape(1, 512),
        eig_time,
    )
    planes = lax.all_to_all(planes, ("lon", "lat"), 0, 0, tiled=True)

    weights, sample = pl.pallas_call(
        backward_kernel,
        out_shape=[shape((64, 16, 256))] * 2,
        in_specs=[VMEM] * 2,
        out_specs=[ANY] * 2,
        scratch_shapes=[
            pltpu.VMEM((2, 256, 1024), BF16),
            pltpu.VMEM((8, 64, 8, 128), F32),
            pltpu.SemaphoreType.DMA((8,)),
        ],
        compiler_params=pltpu.CompilerParams(vmem_limit_bytes=32 * MIB),
        cost_estimate=cost(3 * 2 * 2048 * 256 * 256, 4 * MIB),
        name="time_backward",
    )(planes.reshape(4096, 128), basis_time)
    return weights, sample


def solution(mesh):
    block = P("lon", "lat", None)
    return jax.shard_map(
        on_device,
        mesh=mesh,
        in_specs=(block,) * 3 + (P(),) * 6,
        out_specs=(block, block),
        check_vma=False,
    )
```

```python
import jax
import jax.numpy as jnp
from jax import lax
from jax.experimental import pallas as pl
from jax.experimental.pallas import tpu as pltpu
from jax.sharding import PartitionSpec as P

NOISE_VAR = 0.25
NOISE_STD = 0.5
BF16 = jnp.bfloat16
F32 = jnp.float32
MIB = 1 << 20
VMEM = pl.BlockSpec(memory_space=pltpu.VMEM)
SMEM = pl.BlockSpec(memory_space=pltpu.SMEM)
ANY = pl.BlockSpec(memory_space=pl.ANY)
NN = (((1,), (0,)), ((), ()))
NT = (((1,), (1,)), ((), ()))


def halves(value):
    high = value.astype(BF16)
    low = (value - high.astype(F32)).astype(BF16)
    return high, low


def product(left, right, dims=NN):
    depth = dims[0][1][0]
    return lax.dot_general(
        jnp.concatenate([left[0], left[0], left[1]], axis=1),
        jnp.concatenate([right[0], right[1], right[0]], axis=depth),
        dimension_numbers=dims,
        preferred_element_type=F32,
    )


def interleave(first, second):
    lanes = lax.broadcasted_iota(jnp.int32, first.shape, 1)
    lower = lanes < 64
    return (
        jnp.where(lower, first, pltpu.roll(second, 64, 1)),
        jnp.where(lower, pltpu.roll(first, 64, 1), second),
    )


def forward_kernel(
    obs_hbm, noise_hbm, prior_hbm, time_hbm, out_hbm, bufs, time, field, out_ref, sems, out_sems
):
    time_copy = pltpu.make_async_copy(time_hbm, time, sems.at[12])
    time_copy.start()
    copies = {}
    for source, j_half in ((0, 0), (1, 0), (0, 1), (1, 1), (2, 0), (2, 1)):
        array = (obs_hbm, noise_hbm, prior_hbm)[source]
        for k_half in range(2):
            slot = source * 4 + j_half * 2 + k_half
            copies[slot] = pltpu.make_async_copy(
                array.at[:, pl.ds(j_half * 8, 8), pl.ds(k_half * 128, 128)],
                bufs.at[slot],
                sems.at[slot],
            )
            copies[slot].start()
    time_copy.wait()
    basis = halves(time[...].T)

    sends = []

    def send(part, first=0, count=256, sem=None):
        steps, rows = pl.ds(first, count), pl.ds(part * 8, 8)
        copy = pltpu.make_async_copy(
            out_ref.reshape(256, 24, 128).at[steps, rows, :],
            out_hbm.at[steps, rows, :],
            out_sems.at[part if sem is None else sem],
        )
        copy.start()
        sends.append(copy)

    def rows(slot, jj):
        return bufs.at[slot].reshape(512, 128)[pl.ds(jj, 64, stride=8), :]

    for j_half in range(2):
        for k_half in range(2):
            copies[j_half * 2 + k_half].wait()
            copies[4 + j_half * 2 + k_half].wait()
        for jj in range(8):
            for k_half in range(2):
                obs = rows(j_half * 2 + k_half, jj)
                shifted = obs - NOISE_STD * rows(4 + j_half * 2 + k_half, jj)
                lanes = slice(k_half * 128, (k_half + 1) * 128)
                for f, value in enumerate((obs, shifted)):
                    target = slice(jj * 128 + f * 64, jj * 128 + (f + 1) * 64)
                    high, low = halves(value)
                    field[0, target, lanes] = high
                    field[1, target, lanes] = low
        result = product(basis, (field[0], field[1]), NT)
        for jj in range(8):
            out_ref[pl.ds(j_half * 8 + jj, 256, stride=24), :] = result[:, jj * 128:(jj + 1) * 128]
        send(j_half)

    for slot in range(8, 12):
        copies[slot].wait()
    for k_half in range(2):
        for jj in range(8):
            both = jnp.concatenate([rows(8 + k_half, jj), rows(10 + k_half, jj)], axis=0)
            out_ref[pl.ds(k_half * 3072 + 16 + jj, 128, stride=24), :] = both.T
        send(2, k_half * 128, 128, 2 + k_half)
    for copy in sends:
        copy.wait()


def middle_kernel(
    in_ref, lon_ref, lat_ref, vals_lon, vals_lat, vals_time, out_ref, x_ref, y_ref, prior_ref
):
    latt = halves(lat_ref[...].T)
    fields = (slice(0, 512), slice(512, 1024))

    for p in range(4):
        lanes = slice(p * 128, (p + 1) * 128)
        for block in range(4):
            rows = slice(block * 128, (block + 1) * 128)
            even = slice(p * 64 + block * 8, p * 64 + block * 8 + 8)
            odd = slice(p * 64 + 32 + block * 8, p * 64 + 32 + block * 8 + 8)
            pair = interleave(
                in_ref[even, 0:16, :].reshape(128, 128), in_ref[odd, 0:16, :].reshape(128, 128)
            )
            for f in range(2):
                target = slice(f * 512 + p * 128, f * 512 + (p + 1) * 128)
                x_ref[0, rows, target], x_ref[1, rows, target] = halves(pair[f])
            first, second = interleave(
                in_ref[even, 16:24, :].reshape(64, 128), in_ref[odd, 16:24, :].reshape(64, 128)
            )
            both = jnp.concatenate([first.reshape(8, 8, 128), second.reshape(8, 8, 128)], axis=1)
            prior_ref[rows, lanes] = both.reshape(128, 128)

    result = product(latt, (x_ref[0], x_ref[1]))
    for rows in fields:
        y_ref[0, rows, :], y_ref[1, rows, :] = halves(result[:, rows])

    lon = halves(lon_ref[...])
    hat = product((y_ref[0], y_ref[1]), lon)
    index = lax.axis_index("lon") * 32 + lax.axis_index("lat")
    column = jnp.broadcast_to(vals_lat[...], (512, 512)).T
    spectrum = vals_lon[...] * column * vals_time[index]
    inverse = 1.0 / (spectrum + NOISE_VAR)
    weight_hat = hat[fields[0]] * inverse
    prior_scale = jnp.sqrt(spectrum) * NOISE_VAR * inverse
    sample_hat = prior_scale * prior_ref[...] + spectrum * inverse * hat[fields[1]]
    for rows, value in zip(fields, (weight_hat, sample_hat)):
        y_ref[0, rows, :], y_ref[1, rows, :] = halves(value)

    result = product((y_ref[0], y_ref[1]), lon, NT)
    for rows in fields:
        x_ref[0, :, rows], x_ref[1, :, rows] = halves(result[rows])

    result = product(halves(lat_ref[...]), (x_ref[0], x_ref[1]))
    for p in range(4):
        even, odd = interleave(
            result[:, p * 128:(p + 1) * 128], result[:, 512 + p * 128:512 + (p + 1) * 128]
        )
        out_ref[p * 64:p * 64 + 32] = even.reshape(32, 16, 128)
        out_ref[p * 64 + 32:p * 64 + 64] = odd.reshape(32, 16, 128)


def backward_kernel(in_ref, time_ref, weights_hbm, sample_hbm, field, bufs, sems):
    basis = halves(time_ref[...])
    copies = []
    for j_half in range(2):
        for jj in range(8):
            lanes = slice(jj * 128, (jj + 1) * 128)
            high, low = halves(in_ref[pl.ds(j_half * 8 + jj, 256, stride=16), :])
            field[0, :, lanes] = high
            field[1, :, lanes] = low
        for k_half in range(2):
            left = tuple(half[k_half * 128:(k_half + 1) * 128] for half in basis)
            result = product(left, (field[0], field[1]))
            slots = [f * 4 + j_half * 2 + k_half for f in range(2)]
            blocks = [result[:, jj * 128:(jj + 1) * 128].T for jj in range(8)]
            for f, array in enumerate((weights_hbm, sample_hbm)):
                target = bufs.at[slots[f]].reshape(512, 128)
                for jj in range(8):
                    target[pl.ds(jj, 64, stride=8), :] = blocks[jj][f * 64:(f + 1) * 64]
                copy = pltpu.make_async_copy(
                    bufs.at[slots[f]],
                    array.at[:, pl.ds(j_half * 8, 8), pl.ds(k_half * 128, 128)],
                    sems.at[slots[f]],
                )
                copy.start()
                copies.append(copy)
    for copy in copies:
        copy.wait()


def shape(dims, kind=F32):
    return jax.ShapeDtypeStruct(dims, kind)


def cost(flops, nbytes):
    return pl.CostEstimate(flops=int(flops), bytes_accessed=int(nbytes), transcendentals=0)


def on_device(
    observed, prior_draw, noise_draw, basis_lon, basis_lat, basis_time, eig_lon, eig_lat, eig_time
):
    packed = pl.pallas_call(
        forward_kernel,
        out_shape=shape((256, 24, 128)),
        in_specs=[ANY] * 4,
        out_specs=ANY,
        scratch_shapes=[
            pltpu.VMEM((12, 64, 8, 128), F32),
            pltpu.VMEM((256, 256), F32),
            pltpu.VMEM((2, 1024, 256), BF16),
            pltpu.VMEM((6144, 128), F32),
            pltpu.SemaphoreType.DMA((13,)),
            pltpu.SemaphoreType.DMA((4,)),
        ],
        compiler_params=pltpu.CompilerParams(vmem_limit_bytes=58 * MIB),
        cost_estimate=cost(3 * 2 * 2048 * 256 * 256, 6 * MIB),
        name="time_forward",
    )(observed, noise_draw, prior_draw, basis_time)
    packed = lax.all_to_all(packed, ("lon", "lat"), 0, 0, tiled=True)

    planes = pl.pallas_call(
        middle_kernel,
        out_shape=shape((256, 16, 128)),
        in_specs=[VMEM] * 5 + [SMEM],
        out_specs=VMEM,
        scratch_shapes=[
            pltpu.VMEM((2, 512, 1024), BF16),
            pltpu.VMEM((2, 1024, 512), BF16),
            pltpu.VMEM((512, 512), F32),
        ],
        compiler_params=pltpu.CompilerParams(vmem_limit_bytes=32 * MIB),
        cost_estimate=cost(3 * 2 * 8 * 512**3, 8 * MIB),
        name="middle",
    )(
        packed,
        basis_lon,
        basis_lat,
        eig_lon.reshape(1, 512),
        eig_lat.reshape(1, 512),
        eig_time,
    )
    planes = lax.all_to_all(planes, ("lon", "lat"), 0, 0, tiled=True)

    weights, sample = pl.pallas_call(
        backward_kernel,
        out_shape=[shape((64, 16, 256))] * 2,
        in_specs=[VMEM] * 2,
        out_specs=[ANY] * 2,
        scratch_shapes=[
            pltpu.VMEM((2, 256, 1024), BF16),
            pltpu.VMEM((8, 64, 8, 128), F32),
            pltpu.SemaphoreType.DMA((8,)),
        ],
        compiler_params=pltpu.CompilerParams(vmem_limit_bytes=32 * MIB),
        cost_estimate=cost(3 * 2 * 2048 * 256 * 256, 4 * MIB),
        name="time_backward",
    )(planes.reshape(4096, 128), basis_time)
    return weights, sample


def solution(mesh):
    block = P("lon", "lat", None)
    return jax.shard_map(
        on_device,
        mesh=mesh,
        in_specs=(block,) * 3 + (P(),) * 6,
        out_specs=(block, block),
        check_vma=False,
    )
```
